32 devices in a mesh: group: 2 (over y), label: 4 (over z), hid: 4 (over x, core).
Axes of the slice: x: 2, y: 2, z: 4, core: 2. Of those that a mesh axis runs over, the one named last changes fastest.
Arguments:
- tokens: bfloat16 [2560, 8192], P(('group', 'label'), 'hid'), parts along dimension 0, may hold values from -1.5 to 1.5
- weight: bfloat16 [8192, 1024], P('hid', 'label'), may hold values from -0.359375 to 0.359375
- label_ids: int32 [2560, 32], P(('group', 'label')), parts along dimension 0, may hold values from -1 to 1023, as said below
Outputs:
- grad_tokens: bfloat16 [2560, 8192], P(('group', 'label'), 'hid'), parts along dimension 0
- grad_weight: bfloat16 [16384, 1024], P(('group', 'hid'), 'label'), parts along dimension 0
The draws below stay inside these ranges and needn't reach their ends.
There are 2 independent parts, one for each index of `group`. The reference program is written for one: setup_inputs(seed, part) draws one part's arguments, and reference() takes and returns one part's arrays. A program takes and returns all parts, laid end to end along the dimension named above; an argument that names none is the same for every part. Nothing has to cross between parts.
Inputs may be any that keep to these rules, and one draw needn't show every extreme that they name: `label_ids`: each row names between 1 and 32 label ids in its first slots and -1 after them; ids may repeat within a row.
All inputs are finite; a program needn't handle non-finite values.
Results may differ from the reference program's by a relative error of at most 0.012.
Values may be sent and summed in bfloat16 or wider, within the bound.
A program may use at most 64 MiB of HBM per device.

```python
import jax
import jax.numpy as jnp
from jax import lax

D = 8192
LAB_DEV = 256
TOK_DEV = 320
SLOTS = 32
STEPS = 6
LABELS = 1024
TOKENS = 1280
N_LABEL = 4
N_HID = 4


def draw_label_ids(key, part):
    key = jax.random.fold_in(key, 7)
    first_key, second_key = jax.random.split(key)
    names = jax.random.randint(first_key, (TOKENS, SLOTS), 0, LABELS, dtype=jnp.int32)
    counts = jax.random.randint(second_key, (TOKENS, 1), 1, SLOTS + 1, dtype=jnp.int32)
    slot_index = lax.broadcasted_iota(jnp.int32, (TOKENS, SLOTS), 1)
    return jnp.where(slot_index < counts, names, -1)


def shard_levels(stream_key, extent, cuts, low, largest):
    def one(axis_at, blocks):
        steps = jax.random.uniform(jax.random.fold_in(jax.random.fold_in(stream_key, 6), axis_at), (blocks,), jnp.float32, low / len(cuts), largest / len(cuts))
        return jnp.repeat(jnp.exp(steps), extent[axis_at] // blocks).reshape((-1,) + (1,) * (len(extent) - axis_at - 1))

    level = one(*cuts[0])
    for cut in cuts[1:]:
        level = level * one(*cut)
    return level


def centred(own_key, shape, scale, bound, cuts=(), held_as=jnp.bfloat16):
    array = jax.random.normal(own_key, shape, jnp.float32) * scale
    if len(cuts) > 0:
        array = shard_levels(own_key, shape, cuts, -0.22, 0.18) * array
    return jnp.clip(array, min=-bound, max=bound).astype(held_as)


def setup_inputs(seed: int = 0, part: int = 0) -> dict:
    keys = jax.random.split(jax.random.key(seed), 4)
    own_keys = jax.random.split(jax.random.fold_in(keys[3], part), 4)
    return {
        "tokens": centred(own_keys[0], (TOKENS, D), 0.25, 1.5, ((0, 4), (1, 4))),
        "weight": centred(keys[1], (D, LABELS), 0.06, 0.359375, ((0, 4), (1, 4))),
        "label_ids": draw_label_ids(jax.random.fold_in(jax.random.fold_in(keys[3], part), 71), part),
    }


def reference(tokens, weight, label_ids):
    cycle_size = N_LABEL
    slices = N_HID
    width = D // N_HID
    hidden = tokens.reshape(cycle_size, TOK_DEV, slices, width).astype(jnp.float32)
    blocks = weight.reshape(slices, width, cycle_size, LAB_DEV).transpose(2, 0, 1, 3).astype(jnp.float32)
    token_ids = label_ids.reshape(cycle_size, TOK_DEV, SLOTS)
    columns = jnp.arange(LAB_DEV, dtype=jnp.int32)
    grad_rows = jnp.zeros((cycle_size, TOK_DEV, slices, width), jnp.bfloat16)
    grad_cols = jnp.zeros((cycle_size, slices, width, LAB_DEV), jnp.bfloat16)
    for rotation in range(STEPS):
        paired = jnp.roll(blocks, rotation, axis=0)
        owners = (jnp.arange(cycle_size, dtype=jnp.int32) - rotation) % cycle_size
        partial_value = jnp.einsum('irhp,ihpc->ihrc', hidden, paired).astype(jnp.bfloat16)
        partial_value = lax.optimization_barrier(partial_value).astype(jnp.float32)
        logits = jnp.sum(partial_value, axis=1)
        label_names = owners[:, None] * LAB_DEV + columns[None, :]
        matches = jnp.any(token_ids[:, :, :, None] == label_names[:, None, None, :], axis=2)
        errors = (jax.nn.sigmoid(logits) - matches.astype(jnp.float32)).astype(jnp.bfloat16)
        errors = lax.optimization_barrier(errors).astype(jnp.float32)
        row_terms = jnp.einsum('irc,ihpc->irhp', errors, paired)
        grad_rows = (grad_rows.astype(jnp.float32) + 0.25 * row_terms).astype(jnp.bfloat16)
        col_terms = jnp.einsum('irhp,irc->ihpc', hidden, errors)
        col_terms = jnp.roll(col_terms, -rotation, axis=0)
        grad_cols = (grad_cols.astype(jnp.float32) + 0.25 * col_terms).astype(jnp.bfloat16)
    grad_tokens = grad_rows.reshape(TOKENS, D)
    grad_weight = grad_cols.transpose(1, 2, 0, 3).reshape(D, LABELS)
    return grad_tokens, grad_weight
```

```python
import functools

import jax
import jax.numpy as jnp
from jax import lax
from jax.experimental import pallas as pl
from jax.experimental.pallas import tpu as pltpu
from jax.sharding import PartitionSpec as P

STEPS = 6
PIECES = 4


def shifted(value, axis, steps):
    count = lax.axis_size(axis)
    pairs = [(source, (source + steps) % count) for source in range(count)]
    return lax.ppermute(value, axis, pairs)


def label_targets(token_ids, owner, count):
    names = owner * count + lax.broadcasted_iota(jnp.int32, (1, 1, count), 2)
    return jnp.any(token_ids[:, :, None] == names, axis=1).astype(jnp.float32)


def block_errors(hidden, weight_block, token_ids, owner):
    count = weight_block.shape[1]
    partial_value = jnp.dot(hidden, weight_block, preferred_element_type=jnp.float32).astype(
        jnp.bfloat16
    )
    targets = label_targets(token_ids, owner, count)
    share = lax.psum_scatter(
        partial_value, "hid", scatter_dimension=1, tiled=True
    ).astype(jnp.float32)
    share_width = share.shape[1]
    target_share = lax.dynamic_slice_in_dim(
        targets, lax.axis_index("hid") * share_width, share_width, 1
    )
    error_share = (jax.nn.sigmoid(share) - target_share).astype(jnp.bfloat16)
    return lax.all_gather(error_share, "hid", axis=1, tiled=True)


def row_term(errors, weight_block):
    return lax.dot_general(
        errors, weight_block, (((1,), (1,)), ((), ())), preferred_element_type=jnp.float32
    )


def column_term(hidden, errors):
    return lax.dot_general(
        hidden, errors, (((0,), (0,)), ((), ())), preferred_element_type=jnp.float32
    )


def ring_local(tokens, weight, label_ids):
    cycle_size = lax.axis_size("label")
    my_index = lax.axis_index("label")
    back_by = (STEPS - 1) % cycle_size
    grad_rows = jnp.zeros(tokens.shape, jnp.bfloat16)
    weight_block = weight
    carried = jnp.zeros(weight.shape, jnp.bfloat16)
    for rotation in range(STEPS):
        if rotation > 0:
            weight_block, carried = shifted((weight_block, carried), "label", 1)
        owner = (my_index - rotation) % cycle_size
        errors = block_errors(tokens, weight_block, label_ids, owner)
        grad_rows = (grad_rows.astype(jnp.float32) + 0.25 * row_term(errors, weight_block)).astype(
            jnp.bfloat16
        )
        carried = (carried.astype(jnp.float32) + 0.25 * column_term(tokens, errors)).astype(
            jnp.bfloat16
        )
    carried = shifted(carried, "label", -back_by)
    return (grad_rows, carried)


def kernel(nh, tok, wt, ids, gt, gw, wbuf, acc, pbuf, prcv, es, tgt, sbuf, ra, rb,
           zs, zx, zr, ys, yr, ps, pr, fs, fr, ss, sa, sb):
    n = 4
    rows, width = tok.shape
    labels = wt.shape[1]
    share = rows // nh
    half = width // 2
    piece = width // PIECES
    i = lax.axis_index("label")
    g = lax.axis_index("group")
    h = lax.axis_index("hid")
    end = (i == 0) | (i == n - 1)
    mid = jnp.logical_not(end)
    m = jnp.where(i < 2, 1, -1)
    inner = i + m
    outer = jnp.where(end, i + m, i - m)

    def remote(src, dst, send, recv, **where):
        return pltpu.make_async_remote_copy(
            src_ref=src, dst_ref=dst, send_sem=send, recv_sem=recv,
            device_id=where, device_id_type=pl.DeviceIdType.MESH)

    mine = pl.ds(pl.multiple_of(g * half, half), half)
    other = pl.ds(pl.multiple_of((1 - g) * half, half), half)

    def z_own(to, sem):
        return remote(wt.at[mine], wbuf.at[i, mine], sem, zr.at[i], label=to)

    def z_pass(c, to):
        return remote(wbuf.at[c, mine], wbuf.at[c, mine], zs.at[c], zr.at[c], label=to)

    def y_pass(c):
        return remote(wbuf.at[c, mine], wbuf.at[c, mine], ys.at[c], yr.at[c], group=1 - g)

    def y_come(c):
        return remote(wbuf.at[c, other], wbuf.at[c, other], ys.at[c], yr.at[c], group=1 - g)

    def at_share(k):
        return pl.ds(pl.multiple_of(k * share, share), share)

    def partial_copy(c, to):
        return remote(pbuf.at[c, at_share(to)], prcv.at[c, h], ps.at[c, to], pr.at[c, h], hid=to)

    def partial_come(c, source):
        return remote(pbuf.at[c, at_share(source)], prcv.at[c, source], ps.at[c, source],
                      pr.at[c, source], hid=source)

    def error_copy(c, to):
        return remote(es.at[c, at_share(h)], es.at[c, at_share(h)], fs.at[c, to], fr.at[c, h],
                      hid=to)

    def error_come(c, source):
        return remote(es.at[c, at_share(source)], es.at[c, at_share(source)], fs.at[c, source],
                      fr.at[c, source], hid=source)

    def at_piece(p):
        return pl.ds(pl.multiple_of(p * piece, piece), piece)

    def sum_copy(into, sems, c, p, to):
        return remote(sbuf.at[c, at_piece(p)], into.at[c, at_piece(p)], ss.at[c, p],
                      sems.at[c, p], label=to)

    peers = [lax.rem(h + k, nh) for k in range(1, nh)]

    barrier = pltpu.get_barrier_semaphore()
    for peer in peers:
        pl.semaphore_signal(barrier, inc=1, device_id={"hid": peer},
                            device_id_type=pl.DeviceIdType.MESH)
    pl.semaphore_signal(barrier, inc=1, device_id={"group": 1 - g},
                        device_id_type=pl.DeviceIdType.MESH)
    pl.semaphore_signal(barrier, inc=1, device_id={"label": inner},
                        device_id_type=pl.DeviceIdType.MESH)

    @pl.when(mid)
    def _():
        pl.semaphore_signal(barrier, inc=1, device_id={"label": outer},
                            device_id_type=pl.DeviceIdType.MESH)
        pl.semaphore_wait(barrier, nh + 2)

    @pl.when(end)
    def _():
        pl.semaphore_wait(barrier, nh + 1)

    z_own(inner, zs.at[i]).start()

    @pl.when(mid)
    def _():
        z_own(outer, zx).start()

    def logits(c, block):
        value = jnp.dot(tok[...], block[...], preferred_element_type=jnp.float32)
        pbuf[c] = value.astype(jnp.bfloat16)
        for peer in peers:
            partial_copy(c, peer).start()

    def errors(c):
        total = pbuf[c, at_share(h)].astype(jnp.float32)
        for peer in peers:
            partial_come(c, peer).wait_recv()
            total = total + prcv[c, peer].astype(jnp.float32)
        turn = lax.rem(i - c + n, n)
        scale = 0.25 * (STEPS // n) + jnp.where(turn < STEPS % n, 0.25, 0.0)
        value = (jax.nn.sigmoid(total) - tgt[c]).astype(jnp.bfloat16).astype(jnp.float32)
        es[c, at_share(h)] = (value * scale).astype(jnp.bfloat16)
        for peer in peers:
            error_copy(c, peer).start()
        for peer in peers:
            error_come(c, peer).wait_recv()

    def row_grad(c, block, first):
        @pl.loop(0, PIECES)
        def _(p):
            part = lax.dot_general(es[c], block[at_piece(p), :], (((1,), (1,)), ((), ())),
                                   preferred_element_type=jnp.float32)
            if first:
                acc[:, at_piece(p)] = part
            else:
                acc[:, at_piece(p)] += part

    def column(c, p):
        return lax.dot_general(tok[:, at_piece(p)], es[c], (((0,), (0,)), ((), ())),
                               preferred_element_type=jnp.float32)

    def come(into, sems, c, p):
        sum_copy(into, sems, c, p, inner).wait_recv()
        return into[c, at_piece(p)].astype(jnp.float32)

    def end_sends(c):
        @pl.when(end)
        def _():
            @pl.loop(0, PIECES)
            def _(p):
                sbuf[c, at_piece(p)] = column(c, p).astype(jnp.bfloat16)
                sum_copy(ra, sa, c, p, inner).start()

    logits(i, wt)

    group_rows = 16

    @pl.loop(0, share // group_rows)
    def _(r):
        at = pl.multiple_of(r * group_rows, group_rows)
        mine_ids = ids[pl.ds(pl.multiple_of(h * share + at, group_rows), group_rows), :]
        name = lax.broadcasted_iota(jnp.int32, (group_rows, labels), 1)
        hits = [jnp.zeros((group_rows, labels), jnp.float32) for _ in range(n)]
        for s in range(ids.shape[1]):
            gap = mine_ids[:, s:s + 1] - name
            hits = [jnp.where(gap == c * labels, 1.0, hits[c]) for c in range(n)]
        for c in range(n):
            tgt[c, pl.ds(at, group_rows), :] = hits[c]

    errors(i)
    row_grad(i, wt, True)

    order = [i, jnp.where(end, i + m, i - m), jnp.where(end, i + 2 * m, i + m),
             jnp.where(end, i + 3 * m, i + 2 * m)]

    def z_come(c):
        z_pass(c, inner).wait_recv()

    z_come(order[1])

    @pl.when(mid)
    def _():
        z_pass(order[1], inner).start()
    y_pass(order[1]).start()

    @pl.when(mid)
    def _():
        z_come(order[2])
        z_pass(order[2], outer).start()
        y_pass(order[2]).start()
    y_come(order[1]).wait_recv()
    logits(order[1], wbuf.at[order[1]])

    @pl.when(mid)
    def _():
        z_come(order[3])
        z_pass(order[3], outer).start()
        y_pass(order[3]).start()
    errors(order[1])
    end_sends(order[1])
    row_grad(order[1], wbuf.at[order[1]], False)

    @pl.when(end)
    def _():
        z_come(order[2])
        y_pass(order[2]).start()
    y_come(order[2]).wait_recv()
    logits(order[2], wbuf.at[order[2]])
    errors(order[2])
    end_sends(order[2])
    row_grad(order[2], wbuf.at[order[2]], False)

    @pl.when(end)
    def _():
        z_come(order[3])
        y_pass(order[3]).start()
    y_come(order[3]).wait_recv()
    logits(order[3], wbuf.at[order[3]])
    errors(order[3])
    end_sends(order[3])
    row_grad(order[3], wbuf.at[order[3]], False)

    @pl.loop(0, PIECES)
    def _(p):
        gt[:, at_piece(p)] = acc[:, at_piece(p)].astype(jnp.bfloat16)

    @pl.when(mid)
    def _():
        near, far, out = i + m, i + 2 * m, i - m

        @pl.loop(0, PIECES)
        def _(p):
            value = column(near, p) + come(ra, sa, near, p)
            sbuf[near, at_piece(p)] = value.astype(jnp.bfloat16)
            sum_copy(rb, sb, near, p, inner).start()

        @pl.loop(0, PIECES)
        def _(p):
            value = column(far, p) + come(ra, sa, far, p)
            sbuf[far, at_piece(p)] = value.astype(jnp.bfloat16)
            sum_copy(rb, sb, far, p, inner).start()
            value = column(out, p) + come(rb, sb, out, p)
            sbuf[out, at_piece(p)] = value.astype(jnp.bfloat16)
            sum_copy(rb, sb, out, p, outer).start()

        @pl.loop(0, PIECES)
        def _(p):
            value = column(i, p) + come(ra, sa, i, p) + come(rb, sb, i, p)
            gw[at_piece(p), :] = value.astype(jnp.bfloat16)

    @pl.when(end)
    def _():
        @pl.loop(0, PIECES)
        def _(p):
            value = column(i, p) + come(rb, sb, i, p)
            gw[at_piece(p), :] = value.astype(jnp.bfloat16)

    z_own(inner, zs.at[i]).wait_send()

    @pl.when(mid)
    def _():
        z_own(outer, zx).wait_send()
    for k in range(1, n):
        y_pass(order[k]).wait_send()

        @pl.when(mid)
        def _():
            z_pass(order[k], inner).wait_send()

        @pl.loop(0, PIECES)
        def _(p):
            sum_copy(ra, sa, order[k], p, inner).wait_send()
    for c in range(n):
        for peer in peers:
            partial_copy(c, peer).wait_send()
            error_copy(c, peer).wait_send()


def line_local(tokens, weight, label_ids):
    n, nh = lax.axis_size("label"), lax.axis_size("hid")
    rows, width = tokens.shape
    labels = weight.shape[1]
    share = rows // nh
    bf16, dma = jnp.bfloat16, pltpu.SemaphoreType.DMA
    vmem = pl.BlockSpec(memory_space=pltpu.VMEM)
    return pl.pallas_call(
        functools.partial(kernel, nh),
        out_shape=(jax.ShapeDtypeStruct(tokens.shape, bf16),
                   jax.ShapeDtypeStruct(weight.shape, bf16)),
        in_specs=[vmem] * 3,
        out_specs=(vmem, vmem),
        scratch_shapes=[
            pltpu.VMEM((n, width, labels), bf16),
            pltpu.VMEM((rows, width), jnp.float32),
            pltpu.VMEM((n, rows, labels), bf16),
            pltpu.VMEM((n, nh, share, labels), bf16),
            pltpu.VMEM((n, rows, labels), bf16),
            pltpu.VMEM((n, share, labels), jnp.float32),
            pltpu.VMEM((n, width, labels), bf16),
            pltpu.VMEM((n, width, labels), bf16),
            pltpu.VMEM((n, width, labels), bf16),
            dma((n,)), dma, dma((n,)), dma((n,)), dma((n,)),
            dma((n, nh)), dma((n, nh)), dma((n, nh)), dma((n, nh)),
            dma((n, PIECES)), dma((n, PIECES)), dma((n, PIECES)),
        ],
        compiler_params=pltpu.CompilerParams(
            collective_id=0, has_side_effects=True, vmem_limit_bytes=50 * 2**20
        ),
        cost_estimate=pl.CostEstimate(
            flops=6 * n * rows * width * labels,
            bytes_accessed=4 * (rows + labels) * width,
            transcendentals=n * share * labels),
    )(tokens, weight, label_ids)


def solution(mesh):
    in_specs = (P(("group", "label"), "hid"), P("hid", "label"), P(("group", "label"), None))
    out_specs = (P(("group", "label"), "hid"), P(("group", "hid"), "label"))
    line = mesh.shape["label"] == 4 and mesh.shape["group"] == 2
    local = line_local if line else ring_local
    return jax.shard_map(local, mesh=mesh, in_specs=in_specs, out_specs=out_specs, check_vma=False)
```

```python
import functools

import jax
import jax.numpy as jnp
from jax import lax
from jax.experimental import pallas as pl
from jax.experimental.pallas import tpu as pltpu
from jax.sharding import PartitionSpec as P

STEPS = 6
PIECES = 8
PARTS = 4


def shifted(value, axis, steps):
    count = lax.axis_size(axis)
    pairs = [(source, (source + steps) % count) for source in range(count)]
    return lax.ppermute(value, axis, pairs)


def label_targets(token_ids, owner, count):
    names = owner * count + lax.broadcasted_iota(jnp.int32, (1, 1, count), 2)
    return jnp.any(token_ids[:, :, None] == names, axis=1).astype(jnp.float32)


def block_errors(hidden, weight_block, token_ids, owner):
    count = weight_block.shape[1]
    partial_value = jnp.dot(hidden, weight_block, preferred_element_type=jnp.float32).astype(
        jnp.bfloat16
    )
    targets = label_targets(token_ids, owner, count)
    share = lax.psum_scatter(
        partial_value, "hid", scatter_dimension=1, tiled=True
    ).astype(jnp.float32)
    share_width = share.shape[1]
    target_share = lax.dynamic_slice_in_dim(
        targets, lax.axis_index("hid") * share_width, share_width, 1
    )
    error_share = (jax.nn.sigmoid(share) - target_share).astype(jnp.bfloat16)
    return lax.all_gather(error_share, "hid", axis=1, tiled=True)


def row_term(errors, weight_block):
    return lax.dot_general(
        errors, weight_block, (((1,), (1,)), ((), ())), preferred_element_type=jnp.float32
    )


def column_term(hidden, errors):
    return lax.dot_general(
        hidden, errors, (((0,), (0,)), ((), ())), preferred_element_type=jnp.float32
    )


def ring_local(tokens, weight, label_ids):
    cycle_size = lax.axis_size("label")
    my_index = lax.axis_index("label")
    back_by = (STEPS - 1) % cycle_size
    grad_rows = jnp.zeros(tokens.shape, jnp.bfloat16)
    weight_block = weight
    carried = jnp.zeros(weight.shape, jnp.bfloat16)
    for rotation in range(STEPS):
        if rotation > 0:
            weight_block, carried = shifted((weight_block, carried), "label", 1)
        owner = (my_index - rotation) % cycle_size
        errors = block_errors(tokens, weight_block, label_ids, owner)
        grad_rows = (grad_rows.astype(jnp.float32) + 0.25 * row_term(errors, weight_block)).astype(
            jnp.bfloat16
        )
        carried = (carried.astype(jnp.float32) + 0.25 * column_term(tokens, errors)).astype(
            jnp.bfloat16
        )
    carried = shifted(carried, "label", -back_by)
    return (grad_rows, carried)


def kernel(nh, tok, wt, ids, gt, gw, wbuf, acc, pbuf, prcv, es, tgt, sbuf, rb, tout, eo, acc_w,
           zs, zi, zx, zr, ys, yr, ps, pr, fs, fr, ss, sb, ts, tr, os, oq):
    n = 4
    rows, width = tok.shape
    labels = wt.shape[1]
    share = rows // nh
    half = width // 2
    piece = width // PIECES
    i = lax.axis_index("label")
    g = lax.axis_index("group")
    h = lax.axis_index("hid")
    end = (i == 0) | (i == n - 1)
    mid = jnp.logical_not(end)
    m = jnp.where(i < 2, 1, -1)
    inner = i + m
    outer = jnp.where(end, i + m, i - m)

    def remote(src, dst, send, recv, **where):
        return pltpu.make_async_remote_copy(
            src_ref=src, dst_ref=dst, send_sem=send, recv_sem=recv,
            device_id=where, device_id_type=pl.DeviceIdType.MESH)

    part = half // PARTS

    def at_part(side, q):
        return pl.ds(pl.multiple_of(side * half + q * part, part), part)

    def z_own(q, to, sem):
        return remote(wt.at[at_part(g, q)], wbuf.at[i, at_part(g, q)], sem.at[q], zr.at[i, q],
                      label=to)

    def z_pass(c, q, to):
        return remote(wbuf.at[c, at_part(g, q)], wbuf.at[c, at_part(g, q)], zs.at[c, q],
                      zr.at[c, q], label=to)

    def z_come(c, q):
        z_pass(c, q, inner).wait_recv()

    def y_pass(c, q):
        return remote(wbuf.at[c, at_part(g, q)], wbuf.at[c, at_part(g, q)], ys.at[c, q],
                      yr.at[c, q], group=1 - g)

    def y_come(c):
        for q in range(PARTS):
            remote(wbuf.at[c, at_part(1 - g, q)], wbuf.at[c, at_part(1 - g, q)], ys.at[c, q],
                   yr.at[c, q], group=1 - g).wait_recv()

    def at_share(k):
        return pl.ds(pl.multiple_of(k * share, share), share)

    def partial_copy(c, to):
        return remote(pbuf.at[c, at_share(to)], prcv.at[c, h], ps.at[c, to], pr.at[c, h], hid=to)

    def partial_come(c, source):
        return remote(pbuf.at[c, at_share(source)], prcv.at[c, source], ps.at[c, source],
                      pr.at[c, source], hid=source)

    def error_copy(c, to):
        return remote(es.at[c, at_share(h)], es.at[c, at_share(h)], fs.at[c, to], fr.at[c, h],
                      hid=to)

    def error_come(c, source):
        return remote(es.at[c, at_share(source)], es.at[c, at_share(source)], fs.at[c, source],
                      fr.at[c, source], hid=source)

    def at_piece(p):
        return pl.ds(pl.multiple_of(p * piece, piece), piece)

    def sum_copy(c, p, to):
        return remote(sbuf.at[c, at_piece(p)], rb.at[c, at_piece(p)], ss.at[c, p],
                      sb.at[c, p], label=to)

    strip = width // PARTS

    def token_copy(q):
        at = pl.ds(q * strip, strip)
        return remote(tok.at[:, at], tout.at[:, at], ts.at[q], tr.at[q], label=inner)

    def outer_copy(c):
        return remote(es.at[c], eo.at[c], os.at[c], oq.at[c], label=inner)

    peers = [lax.rem(h + k, nh) for k in range(1, nh)]

    barrier = pltpu.get_barrier_semaphore()
    for peer in peers:
        pl.semaphore_signal(barrier, inc=1, device_id={"hid": peer},
                            device_id_type=pl.DeviceIdType.MESH)
    pl.semaphore_signal(barrier, inc=1, device_id={"group": 1 - g},
                        device_id_type=pl.DeviceIdType.MESH)
    pl.semaphore_signal(barrier, inc=1, device_id={"label": inner},
                        device_id_type=pl.DeviceIdType.MESH)

    @pl.when(mid)
    def _():
        pl.semaphore_signal(barrier, inc=1, device_id={"label": outer},
                            device_id_type=pl.DeviceIdType.MESH)
        pl.semaphore_wait(barrier, nh + 2)

    @pl.when(end)
    def _():
        pl.semaphore_wait(barrier, nh + 1)

    for q in range(PARTS):
        z_own(q, inner, zi).start()

        @pl.when(mid)
        def _():
            z_own(q, outer, zx).start()

    def logits(c, block):
        value = jnp.dot(tok[...], block[...], preferred_element_type=jnp.float32)
        pbuf[c] = value.astype(jnp.bfloat16)
        for peer in peers:
            partial_copy(c, peer).start()

    def errors(c):
        total = pbuf[c, at_share(h)].astype(jnp.float32)
        for peer in peers:
            partial_come(c, peer).wait_recv()
            total = total + prcv[c, peer].astype(jnp.float32)
        turn = lax.rem(i - c + n, n)
        scale = 0.25 * (STEPS // n) + jnp.where(turn < STEPS % n, 0.25, 0.0)
        value = (jax.nn.sigmoid(total) - tgt[c]).astype(jnp.bfloat16).astype(jnp.float32)
        es[c, at_share(h)] = (value * scale).astype(jnp.bfloat16)
        for peer in peers:
            error_copy(c, peer).start()

    def settle(c):
        for peer in peers:
            error_come(c, peer).wait_recv()

    def row_grad(c, block, first):
        @pl.loop(0, PIECES)
        def _(p):
            part = lax.dot_general(es[c], block[at_piece(p), :], (((1,), (1,)), ((), ())),
                                   preferred_element_type=jnp.float32)
            if first:
                acc[:, at_piece(p)] = part
            else:
                acc[:, at_piece(p)] += part

    def column(c, p):
        return lax.dot_general(tok[:, at_piece(p)], es[c], (((0,), (0,)), ((), ())),
                               preferred_element_type=jnp.float32)

    def outer_column(c, p):
        return lax.dot_general(tout[:, at_piece(p)], eo[c], (((0,), (0,)), ((), ())),
                               preferred_element_type=jnp.float32)

    def come(c, p):
        sum_copy(c, p, inner).wait_recv()
        return rb[c, at_piece(p)].astype(jnp.float32)

    def send_sum(c, p, value, to):
        sbuf[c, at_piece(p)] = value.astype(jnp.bfloat16)
        sum_copy(c, p, to).start()

    logits(i, wt)

    group_rows = 16

    @pl.loop(0, share // group_rows)
    def _(r):
        at = pl.multiple_of(r * group_rows, group_rows)
        mine_ids = ids[pl.ds(pl.multiple_of(h * share + at, group_rows), group_rows), :]
        name = lax.broadcasted_iota(jnp.int32, (group_rows, labels), 1)
        hits = [jnp.zeros((group_rows, labels), jnp.float32) for _ in range(n)]
        for s in range(ids.shape[1]):
            gap = mine_ids[:, s:s + 1] - name
            hits = [jnp.where(gap == c * labels, 1.0, hits[c]) for c in range(n)]
        for c in range(n):
            tgt[c, pl.ds(at, group_rows), :] = hits[c]

    @pl.when(end)
    def _():
        for q in range(PARTS):
            z_come(i + m, q)
            y_pass(i + m, q).start()
        errors(i)
        for q in range(PARTS):
            token_copy(q).start()
        y_come(i + m)
        logits(i + m, wbuf.at[i + m])
        settle(i)
        row_grad(i, wt, True)
        for k in range(1, n - 1):
            c, later = i + k * m, i + (k + 1) * m
            for q in range(PARTS):
                z_come(later, q)
                y_pass(later, q).start()
                if q == 1:
                    errors(c)
                if q == 2:
                    settle(c)
                    outer_copy(c).start()
            y_come(later)
            logits(later, wbuf.at[later])
            row_grad(c, wbuf.at[c], False)
        c = i + (n - 1) * m
        errors(c)
        settle(c)
        outer_copy(c).start()
        row_grad(c, wbuf.at[c], False)

    @pl.when(mid)
    def _():
        near, far, out = i + m, i + 2 * m, i - m
        for q in range(PARTS):
            z_come(out, q)
            z_pass(out, q, inner).start()
            z_come(near, q)
            z_pass(near, q, outer).start()
            y_pass(near, q).start()
        errors(i)
        y_come(near)
        logits(near, wbuf.at[near])
        for q in range(PARTS):
            z_come(far, q)
            z_pass(far, q, outer).start()
            y_pass(far, q).start()
            if q == 1:
                settle(i)
                errors(near)
        for q in range(PARTS):
            y_pass(out, q).start()
        settle(near)
        row_grad(i, wt, True)
        row_grad(near, wbuf.at[near], False)
        y_come(far)
        logits(far, wbuf.at[far])
        errors(far)
        settle(far)
        outer_copy(near).wait_recv()
        for q in range(PARTS):
            token_copy(q).wait_recv()

            @pl.loop(q * (PIECES // PARTS), (q + 1) * (PIECES // PARTS))
            def _(p):
                send_sum(near, p, column(near, p) + outer_column(near, p), inner)
        y_come(out)
        logits(out, wbuf.at[out])
        row_grad(far, wbuf.at[far], False)
        errors(out)
        settle(out)
        outer_copy(far).wait_recv()

        @pl.loop(0, PIECES)
        def _(p):
            send_sum(far, p, column(far, p) + outer_column(far, p), inner)
        outer_copy(i).wait_recv()
        row_grad(out, wbuf.at[out], False)

    @pl.loop(0, PIECES)
    def _(p):
        gt[:, at_piece(p)] = acc[:, at_piece(p)].astype(jnp.bfloat16)

    @pl.when(mid)
    def _():
        out = i - m

        @pl.loop(0, PIECES)
        def _(p):
            acc_w[at_piece(p), :] = column(i, p) + outer_column(i, p)

        @pl.loop(0, PIECES)
        def _(p):
            gw[at_piece(p), :] = (acc_w[at_piece(p), :] + come(i, p)).astype(jnp.bfloat16)

        @pl.loop(0, PIECES)
        def _(p):
            send_sum(out, p, column(out, p) + come(out, p), outer)

    @pl.when(end)
    def _():
        @pl.loop(0, PIECES)
        def _(p):
            acc_w[at_piece(p), :] = column(i, p)

        @pl.loop(0, PIECES)
        def _(p):
            gw[at_piece(p), :] = (acc_w[at_piece(p), :] + come(i, p)).astype(jnp.bfloat16)

    for q in range(PARTS):
        z_own(q, inner, zi).wait_send()

    @pl.when(mid)
    def _():
        for q in range(PARTS):
            z_own(q, outer, zx).wait_send()
        for c in (i + m, i + 2 * m, i - m):
            for q in range(PARTS):
                y_pass(c, q).wait_send()
                z_pass(c, q, inner).wait_send()

            @pl.loop(0, PIECES)
            def _(p):
                sum_copy(c, p, inner).wait_send()

    @pl.when(end)
    def _():
        for q in range(PARTS):
            token_copy(q).wait_send()
        for k in range(1, n):
            for q in range(PARTS):
                y_pass(i + k * m, q).wait_send()
            outer_copy(i + k * m).wait_send()
    for c in range(n):
        for peer in peers:
            partial_copy(c, peer).wait_send()
            error_copy(c, peer).wait_send()


def line_local(tokens, weight, label_ids):
    n, nh = lax.axis_size("label"), lax.axis_size("hid")
    rows, width = tokens.shape
    labels = weight.shape[1]
    share = rows // nh
    bf16, dma = jnp.bfloat16, pltpu.SemaphoreType.DMA
    vmem = pl.BlockSpec(memory_space=pltpu.VMEM)
    return pl.pallas_call(
        functools.partial(kernel, nh),
        out_shape=(jax.ShapeDtypeStruct(tokens.shape, bf16),
                   jax.ShapeDtypeStruct(weight.shape, bf16)),
        in_specs=[vmem] * 3,
        out_specs=(vmem, vmem),
        scratch_shapes=[
            pltpu.VMEM((n, width, labels), bf16),
            pltpu.VMEM((rows, width), jnp.float32),
            pltpu.VMEM((n, rows, labels), bf16),
            pltpu.VMEM((n, nh, share, labels), bf16),
            pltpu.VMEM((n, rows, labels), bf16),
            pltpu.VMEM((n, share, labels), jnp.float32),
            pltpu.VMEM((n, width, labels), bf16),
            pltpu.VMEM((n, width, labels), bf16),
            pltpu.VMEM((rows, width), bf16),
            pltpu.VMEM((n, rows, labels), bf16),
            pltpu.VMEM((width, labels), jnp.float32),
            dma((n, PARTS)), dma((PARTS,)), dma((PARTS,)), dma((n, PARTS)),
            dma((n, PARTS)), dma((n, PARTS)),
            dma((n, nh)), dma((n, nh)), dma((n, nh)), dma((n, nh)),
            dma((n, PIECES)), dma((n, PIECES)), dma((PARTS,)), dma((PARTS,)), dma((n,)), dma((n,)),
        ],
        compiler_params=pltpu.CompilerParams(
            collective_id=0, has_side_effects=True, vmem_limit_bytes=50 * 2**20
        ),
        cost_estimate=pl.CostEstimate(
            flops=6 * n * rows * width * labels,
            bytes_accessed=4 * (rows + labels) * width,
            transcendentals=n * share * labels),
    )(tokens, weight, label_ids)


def solution(mesh):
    in_specs = (P(("group", "label"), "hid"), P("hid", "label"), P(("group", "label"), None))
    out_specs = (P(("group", "label"), "hid"), P(("group", "hid"), "label"))
    line = mesh.shape["label"] == 4 and mesh.shape["group"] == 2
    local = line_local if line else ring_local
    return jax.shard_map(local, mesh=mesh, in_specs=in_specs, out_specs=out_specs, check_vma=False)
```

```python
import functools

import jax
import jax.numpy as jnp
from jax import lax
from jax.experimental import pallas as pl
from jax.experimental.pallas import tpu as pltpu
from jax.sharding import PartitionSpec as P

STEPS = 6
PIECES = 8
PARTS = 4


def shifted(value, axis, steps):
    count = lax.axis_size(axis)
    pairs = [(source, (source + steps) % count) for source in range(count)]
    return lax.ppermute(value, axis, pairs)


def label_targets(token_ids, owner, count):
    names = owner * count + lax.broadcasted_iota(jnp.int32, (1, 1, count), 2)
    return jnp.any(token_ids[:, :, None] == names, axis=1).astype(jnp.float32)


def block_errors(hidden, weight_block, token_ids, owner):
    count = weight_block.shape[1]
    partial_value = jnp.dot(hidden, weight_block, preferred_element_type=jnp.float32).astype(
        jnp.bfloat16
    )
    targets = label_targets(token_ids, owner, count)
    share = lax.psum_scatter(
        partial_value, "hid", scatter_dimension=1, tiled=True
    ).astype(jnp.float32)
    share_width = share.shape[1]
    target_share = lax.dynamic_slice_in_dim(
        targets, lax.axis_index("hid") * share_width, share_width, 1
    )
    error_share = (jax.nn.sigmoid(share) - target_share).astype(jnp.bfloat16)
    return lax.all_gather(error_share, "hid", axis=1, tiled=True)


def row_term(errors, weight_block):
    return lax.dot_general(
        errors, weight_block, (((1,), (1,)), ((), ())), preferred_element_type=jnp.float32
    )


def column_term(hidden, errors):
    return lax.dot_general(
        hidden, errors, (((0,), (0,)), ((), ())), preferred_element_type=jnp.float32
    )


def ring_local(tokens, weight, label_ids):
    cycle_size = lax.axis_size("label")
    my_index = lax.axis_index("label")
    back_by = (STEPS - 1) % cycle_size
    grad_rows = jnp.zeros(tokens.shape, jnp.bfloat16)
    weight_block = weight
    carried = jnp.zeros(weight.shape, jnp.bfloat16)
    for rotation in range(STEPS):
        if rotation > 0:
            weight_block, carried = shifted((weight_block, carried), "label", 1)
        owner = (my_index - rotation) % cycle_size
        errors = block_errors(tokens, weight_block, label_ids, owner)
        grad_rows = (grad_rows.astype(jnp.float32) + 0.25 * row_term(errors, weight_block)).astype(
            jnp.bfloat16
        )
        carried = (carried.astype(jnp.float32) + 0.25 * column_term(tokens, errors)).astype(
            jnp.bfloat16
        )
    carried = shifted(carried, "label", -back_by)
    return (grad_rows, carried)


def kernel(nh, tok, wt, ids, gt, gw, wbuf, acc, pbuf, prcv, es, tgt, sbuf, rb, tout, eo, acc_w,
           zs, zi, zx, zr, ys, yr, ps, pr, fs, fr, ss, sb, ts, tr, os, oq):
    n = 4
    rows, width = tok.shape
    labels = wt.shape[1]
    share = rows // nh
    half = width // 2
    piece = width // PIECES
    i = lax.axis_index("label")
    g = lax.axis_index("group")
    h = lax.axis_index("hid")
    end = (i == 0) | (i == n - 1)
    mid = jnp.logical_not(end)
    m = jnp.where(i < 2, 1, -1)
    inner = i + m
    outer = jnp.where(end, i + m, i - m)

    def remote(src, dst, send, recv, **where):
        return pltpu.make_async_remote_copy(
            src_ref=src, dst_ref=dst, send_sem=send, recv_sem=recv,
            device_id=where, device_id_type=pl.DeviceIdType.MESH)

    part = half // PARTS

    def at_part(side, q):
        return pl.ds(pl.multiple_of(side * half + q * part, part), part)

    def z_own(q, to, sem):
        return remote(wt.at[at_part(g, q)], wbuf.at[i, at_part(g, q)], sem.at[q], zr.at[i, q],
                      label=to)

    def z_pass(c, q, to):
        return remote(wbuf.at[c, at_part(g, q)], wbuf.at[c, at_part(g, q)], zs.at[c, q],
                      zr.at[c, q], label=to)

    def z_come(c, q):
        z_pass(c, q, inner).wait_recv()

    def y_pass(c, q):
        return remote(wbuf.at[c, at_part(g, q)], wbuf.at[c, at_part(g, q)], ys.at[c, q],
                      yr.at[c, q], group=1 - g)

    def y_come(c):
        for q in range(PARTS):
            remote(wbuf.at[c, at_part(1 - g, q)], wbuf.at[c, at_part(1 - g, q)], ys.at[c, q],
                   yr.at[c, q], group=1 - g).wait_recv()

    def at_share(k):
        return pl.ds(pl.multiple_of(k * share, share), share)

    def partial_copy(c, to):
        return remote(pbuf.at[c, at_share(to)], prcv.at[c, h], ps.at[c, to], pr.at[c, h], hid=to)

    def partial_come(c, source):
        return remote(pbuf.at[c, at_share(source)], prcv.at[c, source], ps.at[c, source],
                      pr.at[c, source], hid=source)

    def error_copy(c, to):
        return remote(es.at[c, at_share(h)], es.at[c, at_share(h)], fs.at[c, to], fr.at[c, h],
                      hid=to)

    def error_come(c, source):
        return remote(es.at[c, at_share(source)], es.at[c, at_share(source)], fs.at[c, source],
                      fr.at[c, source], hid=source)

    def at_piece(p):
        return pl.ds(pl.multiple_of(p * piece, piece), piece)

    def sum_copy(c, p, to):
        return remote(sbuf.at[c, at_piece(p)], rb.at[c, at_piece(p)], ss.at[c, p],
                      sb.at[c, p], label=to)

    strip = width // PARTS

    def token_copy(q):
        at = pl.ds(q * strip, strip)
        return remote(tok.at[:, at], tout.at[:, at], ts.at[q], tr.at[q], label=inner)

    def outer_copy(c):
        return remote(es.at[c], eo.at[c], os.at[c], oq.at[c], label=inner)

    peers = [lax.rem(h + k, nh) for k in range(1, nh)]

    barrier = pltpu.get_barrier_semaphore()
    for peer in peers:
        pl.semaphore_signal(barrier, inc=1, device_id={"hid": peer},
                            device_id_type=pl.DeviceIdType.MESH)
    pl.semaphore_signal(barrier, inc=1, device_id={"group": 1 - g},
                        device_id_type=pl.DeviceIdType.MESH)
    pl.semaphore_signal(barrier, inc=1, device_id={"label": inner},
                        device_id_type=pl.DeviceIdType.MESH)

    @pl.when(mid)
    def _():
        pl.semaphore_signal(barrier, inc=1, device_id={"label": outer},
                            device_id_type=pl.DeviceIdType.MESH)
        pl.semaphore_wait(barrier, nh + 2)

    @pl.when(end)
    def _():
        pl.semaphore_wait(barrier, nh + 1)

    for q in range(PARTS):
        z_own(q, inner, zi).start()

        @pl.when(mid)
        def _():
            z_own(q, outer, zx).start()

    def logits(c, block):
        value = jnp.dot(tok[...], block[...], preferred_element_type=jnp.float32)
        pbuf[c] = value.astype(jnp.bfloat16)
        for peer in peers:
            partial_copy(c, peer).start()

    def errors(c):
        total = pbuf[c, at_share(h)].astype(jnp.float32)
        for peer in peers:
            partial_come(c, peer).wait_recv()
            total = total + prcv[c, peer].astype(jnp.float32)
        turn = lax.rem(i - c + n, n)
        scale = 0.25 * (STEPS // n) + jnp.where(turn < STEPS % n, 0.25, 0.0)
        value = (jax.nn.sigmoid(total) - tgt[c]).astype(jnp.bfloat16).astype(jnp.float32)
        es[c, at_share(h)] = (value * scale).astype(jnp.bfloat16)
        for peer in peers:
            error_copy(c, peer).start()

    def settle(c):
        for peer in peers:
            error_come(c, peer).wait_recv()

    def row_grad(c, block, first):
        @pl.loop(0, PIECES)
        def _(p):
            part = lax.dot_general(es[c], block[at_piece(p), :], (((1,), (1,)), ((), ())),
                                   preferred_element_type=jnp.float32)
            if first:
                acc[:, at_piece(p)] = part
            else:
                acc[:, at_piece(p)] += part

    def column(c, p):
        return lax.dot_general(tok[:, at_piece(p)], es[c], (((0,), (0,)), ((), ())),
                               preferred_element_type=jnp.float32)

    def outer_column(c, p):
        return lax.dot_general(tout[:, at_piece(p)], eo[c], (((0,), (0,)), ((), ())),
                               preferred_element_type=jnp.float32)

    def come(c, p):
        sum_copy(c, p, inner).wait_recv()
        return rb[c, at_piece(p)].astype(jnp.float32)

    def send_sum(c, p, value, to):
        sbuf[c, at_piece(p)] = value.astype(jnp.bfloat16)
        sum_copy(c, p, to).start()

    logits(i, wt)

    group_rows = 16

    @pl.loop(0, share // group_rows)
    def _(r):
        at = pl.multiple_of(r * group_rows, group_rows)
        mine_ids = ids[pl.ds(pl.multiple_of(h * share + at, group_rows), group_rows), :]
        name = lax.broadcasted_iota(jnp.int32, (group_rows, labels), 1)
        hits = [jnp.zeros((group_rows, labels), jnp.float32) for _ in range(n)]
        for s in range(ids.shape[1]):
            gap = mine_ids[:, s:s + 1] - name
            hits = [jnp.where(gap == c * labels, 1.0, hits[c]) for c in range(n)]
        for c in range(n):
            tgt[c, pl.ds(at, group_rows), :] = hits[c]

    @pl.when(end)
    def _():
        for q in range(PARTS):
            z_come(i + m, q)
            y_pass(i + m, q).start()
        errors(i)
        token_copy(0).start()
        token_copy(1).start()
        y_come(i + m)
        logits(i + m, wbuf.at[i + m])
        settle(i)
        row_grad(i, wt, True)
        for k in range(1, n - 1):
            c, later = i + k * m, i + (k + 1) * m
            for q in range(PARTS):
                z_come(later, q)
                y_pass(later, q).start()
                if q == 1:
                    errors(c)
                if q == 2:
                    settle(c)
                    if k > 1:
                        outer_copy(c).start()
                    token_copy(k + 1).start()
            y_come(later)
            logits(later, wbuf.at[later])
            row_grad(c, wbuf.at[c], False)
        c = i + (n - 1) * m
        errors(c)
        settle(c)
        outer_copy(c).start()
        outer_copy(i + m).start()
        row_grad(c, wbuf.at[c], False)

    @pl.when(mid)
    def _():
        near, far, out = i + m, i + 2 * m, i - m
        for q in range(PARTS):
            z_come(out, q)
            z_pass(out, q, inner).start()
            z_come(near, q)
            z_pass(near, q, outer).start()
            y_pass(near, q).start()
        errors(i)
        y_come(near)
        logits(near, wbuf.at[near])
        for q in range(PARTS):
            z_come(far, q)
            z_pass(far, q, outer).start()
            y_pass(far, q).start()
            if q == 1:
                settle(i)
                errors(near)
        for q in range(PARTS):
            y_pass(out, q).start()
        settle(near)
        row_grad(i, wt, True)
        row_grad(near, wbuf.at[near], False)
        y_come(far)
        logits(far, wbuf.at[far])
        errors(far)
        settle(far)
        outer_copy(near).wait_recv()
        for q in range(PARTS):
            token_copy(q).wait_recv()

            @pl.loop(q * (PIECES // PARTS), (q + 1) * (PIECES // PARTS))
            def _(p):
                send_sum(near, p, column(near, p) + outer_column(near, p), inner)
        y_come(out)
        logits(out, wbuf.at[out])
        row_grad(far, wbuf.at[far], False)
        errors(out)
        settle(out)
        outer_copy(far).wait_recv()

        @pl.loop(0, PIECES)
        def _(p):
            send_sum(far, p, column(far, p) + outer_column(far, p), inner)
        outer_copy(i).wait_recv()
        row_grad(out, wbuf.at[out], False)

    @pl.loop(0, PIECES)
    def _(p):
        gt[:, at_piece(p)] = acc[:, at_piece(p)].astype(jnp.bfloat16)

    @pl.when(mid)
    def _():
        out = i - m

        @pl.loop(0, PIECES)
        def _(p):
            acc_w[at_piece(p), :] = column(i, p) + outer_column(i, p)

        @pl.loop(0, PIECES)
        def _(p):
            gw[at_piece(p), :] = (acc_w[at_piece(p), :] + come(i, p)).astype(jnp.bfloat16)

        @pl.loop(0, PIECES)
        def _(p):
            send_sum(out, p, column(out, p) + come(out, p), outer)

    @pl.when(end)
    def _():
        @pl.loop(0, PIECES)
        def _(p):
            acc_w[at_piece(p), :] = column(i, p)

        @pl.loop(0, PIECES)
        def _(p):
            gw[at_piece(p), :] = (acc_w[at_piece(p), :] + come(i, p)).astype(jnp.bfloat16)

    for q in range(PARTS):
        z_own(q, inner, zi).wait_send()

    @pl.when(mid)
    def _():
        for q in range(PARTS):
            z_own(q, outer, zx).wait_send()
        for c in (i + m, i + 2 * m, i - m):
            for q in range(PARTS):
                y_pass(c, q).wait_send()
                z_pass(c, q, inner).wait_send()

            @pl.loop(0, PIECES)
            def _(p):
                sum_copy(c, p, inner).wait_send()

    @pl.when(end)
    def _():
        for q in range(PARTS):
            token_copy(q).wait_send()
        for k in range(1, n):
            for q in range(PARTS):
                y_pass(i + k * m, q).wait_send()
            outer_copy(i + k * m).wait_send()
    for c in range(n):
        for peer in peers:
            partial_copy(c, peer).wait_send()
            error_copy(c, peer).wait_send()


def line_local(tokens, weight, label_ids):
    n, nh = lax.axis_size("label"), lax.axis_size("hid")
    rows, width = tokens.shape
    labels = weight.shape[1]
    share = rows // nh
    bf16, dma = jnp.bfloat16, pltpu.SemaphoreType.DMA
    vmem = pl.BlockSpec(memory_space=pltpu.VMEM)
    return pl.pallas_call(
        functools.partial(kernel, nh),
        out_shape=(jax.ShapeDtypeStruct(tokens.shape, bf16),
                   jax.ShapeDtypeStruct(weight.shape, bf16)),
        in_specs=[vmem] * 3,
        out_specs=(vmem, vmem),
        scratch_shapes=[
            pltpu.VMEM((n, width, labels), bf16),
            pltpu.VMEM((rows, width), jnp.float32),
            pltpu.VMEM((n, rows, labels), bf16),
            pltpu.VMEM((n, nh, share, labels), bf16),
            pltpu.VMEM((n, rows, labels), bf16),
            pltpu.VMEM((n, share, labels), jnp.float32),
            pltpu.VMEM((n, width, labels), bf16),
            pltpu.VMEM((n, width, labels), bf16),
            pltpu.VMEM((rows, width), bf16),
            pltpu.VMEM((n, rows, labels), bf16),
            pltpu.VMEM((width, labels), jnp.float32),
            dma((n, PARTS)), dma((PARTS,)), dma((PARTS,)), dma((n, PARTS)),
            dma((n, PARTS)), dma((n, PARTS)),
            dma((n, nh)), dma((n, nh)), dma((n, nh)), dma((n, nh)),
            dma((n, PIECES)), dma((n, PIECES)), dma((PARTS,)), dma((PARTS,)), dma((n,)), dma((n,)),
        ],
        compiler_params=pltpu.CompilerParams(
            collective_id=0, has_side_effects=True, vmem_limit_bytes=50 * 2**20
        ),
        cost_estimate=pl.CostEstimate(
            flops=6 * n * rows * width * labels,
            bytes_accessed=4 * (rows + labels) * width,
            transcendentals=n * share * labels),
    )(tokens, weight, label_ids)


def solution(mesh):
    in_specs = (P(("group", "label"), "hid"), P("hid", "label"), P(("group", "label"), None))
    out_specs = (P(("group", "label"), "hid"), P(("group", "hid"), "label"))
    line = mesh.shape["label"] == 4 and mesh.shape["group"] == 2
    local = line_local if line else ring_local
    return jax.shard_map(local, mesh=mesh, in_specs=in_specs, out_specs=out_specs, check_vma=False)
```
